32 devices in a mesh: ctx: 16 (over z, x, core), head: 2 (over y).
Axes of the slice: x: 2, y: 2, z: 4, core: 2. Of those that a mesh axis runs over, the one named last changes fastest.
Arguments:
- query_head_rows: bfloat16 [4096, 4096], P('ctx', 'head'), may hold values from -4 to 4
- key_head_rows: bfloat16 [4096, 1024], P('ctx', 'head'), may hold values from -4 to 4
- value_head_rows: bfloat16 [4096, 1024], P('ctx', 'head'), may hold values from -4 to 4
- forward_output: bfloat16 [4096, 4096], P('ctx', 'head'), may hold values from -4 to 4, as said below
- cotangent: bfloat16 [4096, 4096], P('ctx', 'head'), may hold values from -6 to 6
- logsumexp: float32 [32, 4096], P('head', 'ctx'), as said below
- document_lengths: int32 [16], replicated, may hold values from 1 to 768, as said below
- linear_row_index: int32 [4096], replicated, may hold values from 0 to 4095, as said below
Outputs:
- query_gradient: bfloat16 [4096, 4096], P(('ctx', 'head'))
- linear_key_gradient: bfloat16 [4096, 1024], P(('ctx', 'head'))
- linear_value_gradient: bfloat16 [4096, 1024], P(('ctx', 'head'))
The draws below stay inside these ranges and needn't reach their ends.
Inputs may be any that keep to these rules, and one draw needn't show every extreme that they name: `logsumexp`: for each head and position, the log of the sum of exp(scores) over the keys that the position sees, from the forward pass on these query_head_rows and key_head_rows. `forward_output`: for each head, the forward pass's softmax weights times value_head_rows, rounded to bfloat16. `document_lengths`: the lengths sum to 4096; the longest document has exactly 768 tokens. `linear_row_index`: A permutation of the 4096 positions. Counting positions in blocks of 256, from one block of the packed sequence at most 32 rows go to one block of linear positions, some pair of blocks reaches 32, and every linear block receives 256 rows.
All inputs are finite; a program needn't handle non-finite values.
Results may differ from the reference program's by a relative error of at most 0.0049.
Values may be sent and summed in bfloat16 or wider, within the bound.
A program may use at most 64 MiB of HBM per device.

```python
import jax
import jax.numpy as jnp
from jax import lax

QUERY_HEADS = 32
KEY_VALUE_HEADS = 8
HEAD_SIZE = 128
TOK_DEV = 256
DOC_BLOCKS = 3
PACKED_TOKENS = 4096
DOC = 768
NDOCS = 16
CAP = 32


def base_fields(key):
    field_keys = jax.random.split(jax.random.fold_in(key, 11), 4)
    document_spans = ((PACKED_TOKENS, QUERY_HEADS * HEAD_SIZE), (PACKED_TOKENS, KEY_VALUE_HEADS * HEAD_SIZE), (PACKED_TOKENS, KEY_VALUE_HEADS * HEAD_SIZE))
    fields = []
    for which in range(3):
        extent = document_spans[which]
        values = jnp.clip(jax.random.normal(field_keys[which], extent, jnp.float32), -4.0, 4.0)
        rounded = lax.optimization_barrier(values.astype(jnp.bfloat16)).astype(jnp.float32)
        fields.append(rounded)
    return fields


def length_draw(key):
    first_key, second_key = jax.random.split(key)
    spare = PACKED_TOKENS - DOC - (NDOCS - 1)
    weights = jax.random.randint(first_key, (NDOCS - 1,), 500, 1001).astype(jnp.int32)
    base = (1 + spare * weights // jnp.sum(weights)).astype(jnp.int32)
    short = PACKED_TOKENS - DOC - jnp.sum(base)
    base = base + (lax.iota(jnp.int32, NDOCS - 1) < short).astype(jnp.int32)
    chosen = jax.random.randint(second_key, (), 0, NDOCS)
    index = lax.iota(jnp.int32, NDOCS)
    source = jnp.clip(jnp.where(index < chosen, index, index - 1), 0, NDOCS - 2)
    return jnp.where(index == chosen, DOC, base[source]).astype(jnp.int32)


def attention_stats(key):
    query_full_rows, key_full_rows, value_full_rows = base_fields(key)
    lengths = length_draw(jax.random.fold_in(key, 5))
    query_groups = QUERY_HEADS // KEY_VALUE_HEADS
    scaling = HEAD_SIZE ** (-0.5)
    spare_border = DOC_BLOCKS * TOK_DEV
    window = spare_border + TOK_DEV
    finish = jnp.cumsum(lengths).astype(jnp.int32)
    firsts = finish - lengths
    positions = lax.iota(jnp.int32, PACKED_TOKENS)
    begins = jnp.max(jnp.where(firsts[None, :] <= positions[:, None], firsts[None, :], 0), axis=1)
    query_vectors = query_full_rows.reshape(PACKED_TOKENS, KEY_VALUE_HEADS, query_groups, HEAD_SIZE)
    padding_width = jnp.zeros((spare_border, KEY_VALUE_HEADS, HEAD_SIZE), jnp.float32)
    key_padded = jnp.concatenate([padding_width, key_full_rows.reshape(PACKED_TOKENS, KEY_VALUE_HEADS, HEAD_SIZE)], axis=0)
    value_padded = jnp.concatenate([padding_width, value_full_rows.reshape(PACKED_TOKENS, KEY_VALUE_HEADS, HEAD_SIZE)], axis=0)

    def one_block(block):
        first = (block * TOK_DEV).astype(jnp.int32)
        query_part = lax.dynamic_slice_in_dim(query_vectors, first, TOK_DEV)
        begin_part = lax.dynamic_slice_in_dim(begins, first, TOK_DEV)
        key_part = lax.dynamic_slice_in_dim(key_padded, first, window)
        value_part = lax.dynamic_slice_in_dim(value_padded, first, window)
        key_pos = first - spare_border + lax.iota(jnp.int32, window)
        query_pos = first + lax.iota(jnp.int32, TOK_DEV)
        visible = (key_pos[None, :] <= query_pos[:, None]) & (key_pos[None, :] >= begin_part[:, None])
        scores = jnp.einsum('qngd,knd->qngk', query_part, key_part) * scaling
        masked = jnp.where(visible[:, None, None, :], scores, -jnp.inf)
        top = jnp.max(masked, axis=3, keepdims=True)
        log_normalizer = top[..., 0] + jnp.log(jnp.sum(jnp.exp(masked - top), axis=3))
        weights = jnp.exp(masked - log_normalizer[..., None])
        outputs = jnp.einsum('qngk,knd->qngd', weights, value_part)
        return (log_normalizer, outputs)
    log_totals, outputs = lax.map(one_block, jnp.arange(PACKED_TOKENS // TOK_DEV, dtype=jnp.int32))
    return (log_totals.reshape(PACKED_TOKENS, QUERY_HEADS).T, outputs.reshape(PACKED_TOKENS, QUERY_HEADS * HEAD_SIZE))


def remap_draw(key):
    count = PACKED_TOKENS // TOK_DEV
    half = CAP // 2
    keys = jax.random.split(key, 5)
    shifts = jax.random.randint(keys[0], (count // 2,), -half, half + 1).astype(jnp.int32)
    shifts = shifts.at[0].set(half)
    loads = jnp.stack([half + shifts, half - shifts], axis=1).reshape(count)
    loads = loads[jax.random.permutation(keys[1], count)]
    labels = jax.random.permutation(keys[2], count).astype(jnp.int32)
    matrix = loads[(labels[None, :] - labels[:, None]) % count].astype(jnp.int32)
    inclusive = jnp.cumsum(matrix, axis=1).astype(jnp.int32)
    exclusive = inclusive - matrix
    places = lax.iota(jnp.int32, TOK_DEV)
    owner_of = jnp.sum((places[None, :, None] >= inclusive[:, None, :]).astype(jnp.int32), axis=2)
    ranks = places[None, :] - jnp.take_along_axis(exclusive, owner_of, axis=1)
    arrivals = (jnp.cumsum(matrix, axis=0) - matrix).astype(jnp.int32)
    slot_at = jnp.take_along_axis(arrivals, owner_of, axis=1) + ranks
    receive_order = jax.vmap(lambda sub: jax.random.permutation(sub, TOK_DEV))(jax.random.split(keys[3], count)).astype(jnp.int32)
    send_order = jax.vmap(lambda sub: jax.random.permutation(sub, TOK_DEV))(jax.random.split(keys[4], count)).astype(jnp.int32)
    position = receive_order[owner_of, slot_at]
    targets = owner_of * TOK_DEV + position
    sources = lax.iota(jnp.int32, count)[:, None] * TOK_DEV + send_order
    return jnp.zeros((PACKED_TOKENS,), jnp.int32).at[sources.reshape(-1)].set(targets.reshape(-1).astype(jnp.int32))


def draw_query_head_rows(key, part):
    return base_fields(key)[0].astype(jnp.bfloat16)


def draw_key_head_rows(key, part):
    return base_fields(key)[1].astype(jnp.bfloat16)


def draw_value_head_rows(key, part):
    return base_fields(key)[2].astype(jnp.bfloat16)


def draw_logsumexp(key, part):
    return attention_stats(key)[0].astype(jnp.float32)


def draw_forward_output(key, part):
    return attention_stats(key)[1].astype(jnp.bfloat16)


def draw_document_lengths(key, part):
    return length_draw(jax.random.fold_in(key, 5)).astype(jnp.int32)


def draw_linear_row_index(key, part):
    return remap_draw(jax.random.fold_in(key, 3)).astype(jnp.int32)


def levels(key, dims, pieces, least, high):
    def one(axis_at, parts):
        draws = jax.random.uniform(jax.random.fold_in(jax.random.fold_in(key, 6), axis_at), (parts,), jnp.float32, least / len(pieces), high / len(pieces))
        return jnp.repeat(jnp.exp(draws), dims[axis_at] // parts).reshape((-1,) + (1,) * (len(dims) - axis_at - 1))

    level = one(*pieces[0])
    for cut in pieces[1:]:
        level = level * one(*cut)
    return level


def normal_values(stream_key, shape, width, bound, cuts=(), kind=jnp.bfloat16):
    values = width * jax.random.normal(stream_key, shape, jnp.float32)
    if cuts:
        values = values * levels(stream_key, shape, cuts, -0.22, 0.18)
    return jnp.clip(values, -bound, bound).astype(kind)


def setup_inputs(seed: int = 0) -> dict:
    key_list = jax.random.split(jax.random.key(seed), 9)
    return {
        "query_head_rows": draw_query_head_rows(jax.random.fold_in(key_list[8], 71), 0),
        "key_head_rows": draw_key_head_rows(jax.random.fold_in(key_list[8], 71), 0),
        "value_head_rows": draw_value_head_rows(jax.random.fold_in(key_list[8], 71), 0),
        "forward_output": draw_forward_output(jax.random.fold_in(key_list[8], 71), 0),
        "cotangent": normal_values(key_list[4], (PACKED_TOKENS, QUERY_HEADS * HEAD_SIZE), 1.0, 6.0, ((0, 16), (1, 2))),
        "logsumexp": draw_logsumexp(jax.random.fold_in(key_list[8], 71), 0),
        "document_lengths": draw_document_lengths(jax.random.fold_in(key_list[8], 71), 0),
        "linear_row_index": draw_linear_row_index(jax.random.fold_in(key_list[8], 71), 0),
    }


def document_begins(document_lengths, positions):
    finish = jnp.cumsum(document_lengths).astype(jnp.int32)
    firsts = (finish - document_lengths).astype(jnp.int32)
    chosen = jnp.where(firsts[None, :] <= positions[:, None], firsts[None, :], 0)
    return jnp.max(chosen, axis=1).astype(jnp.int32)


def reference(query_head_rows, key_head_rows, value_head_rows, forward_output, cotangent, logsumexp, document_lengths, linear_row_index):
    query_groups = QUERY_HEADS // KEY_VALUE_HEADS
    scaling = HEAD_SIZE ** -0.5
    spare_border = DOC_BLOCKS * TOK_DEV
    window = spare_border + TOK_DEV
    positions = lax.iota(jnp.int32, PACKED_TOKENS)
    begins = document_begins(document_lengths, positions)
    query_vectors = query_head_rows.astype(jnp.float32).reshape(PACKED_TOKENS, KEY_VALUE_HEADS, query_groups, HEAD_SIZE)
    output_gradient = cotangent.astype(jnp.float32).reshape(PACKED_TOKENS, KEY_VALUE_HEADS, query_groups, HEAD_SIZE)
    log_normalizer = logsumexp.T.reshape(PACKED_TOKENS, KEY_VALUE_HEADS, query_groups)
    row_correction = jnp.sum(output_gradient * forward_output.astype(jnp.float32).reshape(PACKED_TOKENS, KEY_VALUE_HEADS, query_groups, HEAD_SIZE), axis=3)
    padding_width = jnp.zeros((spare_border, KEY_VALUE_HEADS, HEAD_SIZE), jnp.float32)
    key_padded = jnp.concatenate([padding_width, key_head_rows.astype(jnp.float32).reshape(PACKED_TOKENS, KEY_VALUE_HEADS, HEAD_SIZE)], axis=0)
    value_padded = jnp.concatenate([padding_width, value_head_rows.astype(jnp.float32).reshape(PACKED_TOKENS, KEY_VALUE_HEADS, HEAD_SIZE)], axis=0)

    def one_block(carry, block):
        key_running_sum, value_running_sum = carry
        first = (block * TOK_DEV).astype(jnp.int32)
        query_part = lax.dynamic_slice_in_dim(query_vectors, first, TOK_DEV)
        grad_part = lax.dynamic_slice_in_dim(output_gradient, first, TOK_DEV)
        total_part = lax.dynamic_slice_in_dim(log_normalizer, first, TOK_DEV)
        delta_part = lax.dynamic_slice_in_dim(row_correction, first, TOK_DEV)
        begin_part = lax.dynamic_slice_in_dim(begins, first, TOK_DEV)
        key_part = lax.dynamic_slice_in_dim(key_padded, first, window)
        value_part = lax.dynamic_slice_in_dim(value_padded, first, window)
        key_pos = first - spare_border + lax.iota(jnp.int32, window)
        query_pos = first + lax.iota(jnp.int32, TOK_DEV)
        visible = (key_pos[None, :] <= query_pos[:, None]) & (key_pos[None, :] >= begin_part[:, None])
        scores = jnp.einsum("qngd,knd->qngk", query_part, key_part) * scaling
        weights = jnp.exp(jnp.where(visible[:, None, None, :], scores - total_part[..., None], -jnp.inf))
        weights_low = lax.optimization_barrier(weights.astype(jnp.bfloat16)).astype(jnp.float32)
        grad_weights = jnp.einsum("qngd,knd->qngk", grad_part, value_part)
        grad_scores = (weights * (grad_weights - delta_part[..., None]) * scaling).astype(jnp.bfloat16)
        grad_scores = lax.optimization_barrier(grad_scores).astype(jnp.float32)
        query_term = jnp.einsum("qngk,knd->qngd", grad_scores, key_part)
        key_term = jnp.einsum("qngk,qngd->knd", grad_scores, query_part)
        value_term = jnp.einsum("qngk,qngd->knd", weights_low, grad_part)
        key_running_sum = lax.dynamic_update_slice_in_dim(key_running_sum, lax.dynamic_slice_in_dim(key_running_sum, first, window) + key_term, first, 0)
        value_running_sum = lax.dynamic_update_slice_in_dim(value_running_sum, lax.dynamic_slice_in_dim(value_running_sum, first, window) + value_term, first, 0)
        return (key_running_sum, value_running_sum), query_term.astype(jnp.bfloat16)

    start_running_sum = jnp.zeros((PACKED_TOKENS + spare_border, KEY_VALUE_HEADS, HEAD_SIZE), jnp.float32)
    block_ids = jnp.arange(PACKED_TOKENS // TOK_DEV, dtype=jnp.int32)
    (key_running_sum, value_running_sum), query_blocks = lax.scan(one_block, (start_running_sum, start_running_sum), block_ids)
    query_grad = query_blocks.reshape(PACKED_TOKENS, QUERY_HEADS * HEAD_SIZE)
    key_row_gradient = key_running_sum[spare_border:].reshape(PACKED_TOKENS, KEY_VALUE_HEADS * HEAD_SIZE).astype(jnp.bfloat16)
    value_row_gradient = value_running_sum[spare_border:].reshape(PACKED_TOKENS, KEY_VALUE_HEADS * HEAD_SIZE).astype(jnp.bfloat16)
    query_gradient = jnp.zeros((PACKED_TOKENS, QUERY_HEADS * HEAD_SIZE), jnp.bfloat16).at[linear_row_index].set(query_grad)
    linear_key_gradient = jnp.zeros((PACKED_TOKENS, KEY_VALUE_HEADS * HEAD_SIZE), jnp.bfloat16).at[linear_row_index].set(key_row_gradient)
    linear_value_gradient = jnp.zeros((PACKED_TOKENS, KEY_VALUE_HEADS * HEAD_SIZE), jnp.bfloat16).at[linear_row_index].set(value_row_gradient)
    return (query_gradient, linear_key_gradient, linear_value_gradient)
```

```python
import functools

import jax
import jax.numpy as jnp
from jax import lax
from jax.experimental import pallas as pl
from jax.experimental.pallas import tpu as pltpu
from jax.sharding import PartitionSpec as P

HEAD_SIZE = 128
DOC_BLOCKS = 3
MESH = pl.DeviceIdType.MESH
NT = (((1,), (1,)), ((), ()))
TN = (((0,), (0,)), ((), ()))
LOG2E = 1.4426950408889634


def kernel(
    blocks,
    heads,
    cap,
    q_ref,
    k_ref,
    v_ref,
    o_ref,
    do_ref,
    lse_ref,
    lens_ref,
    lri_ref,
    outq_ref,
    outk_ref,
    outv_ref,
    kv_in,
    bias,
    send_pick,
    land_t,
    land_pick,
    part_out,
    part_in,
    own_part,
    q_out,
    q_in,
    kv_out,
    kv_back,
    hq,
    hkv,
    kv_ssem,
    kv_rsem,
    part_ssem,
    part_rsem,
    row_ssem,
    row_rsem,
    head_ssem,
    head_rsem,
):
    length, d = q_ref.shape[0], HEAD_SIZE
    kv_heads = k_ref.shape[1] // d
    width = q_ref.shape[1] // kv_heads
    groups = width // d
    kv_cols = kv_heads * d
    slots = blocks * cap
    out_rows = length // heads
    scale = d**-0.5
    me = lax.axis_index("ctx")
    my_head = lax.axis_index("head")
    f32, bf16 = jnp.float32, jnp.bfloat16

    def peer(by):
        return lax.rem(me + by + blocks, blocks)

    barrier = pltpu.get_barrier_semaphore()

    def greet(s, _):
        pl.semaphore_signal(barrier, inc=1, device_id=(peer(s), my_head), device_id_type=MESH)
        return 0

    def greet_head(s, _):
        pl.semaphore_signal(
            barrier, inc=1, device_id=(me, lax.rem(my_head + s, heads)), device_id_type=MESH
        )
        return 0

    lax.fori_loop(1, blocks, greet, 0)
    lax.fori_loop(1, heads, greet_head, 0)
    pl.semaphore_wait(barrier, blocks - 1 + heads - 1)

    def cols(n, size):
        return pl.ds(pl.multiple_of(n * size, size), size)

    def kv_copy(n, dist, which):
        source = (k_ref, v_ref)[which]
        return pltpu.make_async_remote_copy(
            src_ref=source.at[:, cols(n, d)],
            dst_ref=kv_in.at[n, dist - 1, which],
            send_sem=kv_ssem.at[n, dist - 1, which],
            recv_sem=kv_rsem.at[n, dist - 1, which],
            device_id=(peer(dist), my_head),
            device_id_type=MESH,
        )

    def part_copy(n, dist, which):
        return pltpu.make_async_remote_copy(
            src_ref=part_out.at[n, dist - 1, which],
            dst_ref=part_in.at[n, dist - 1, which],
            send_sem=part_ssem.at[n, dist - 1, which],
            recv_sem=part_rsem.at[n, dist - 1, which],
            device_id=(peer(-dist), my_head),
            device_id_type=MESH,
        )

    def slot_rows(block):
        return pl.ds(pl.multiple_of(block * cap, cap), cap)

    def row_copy(stage, s, dst_block):
        to = peer(s)
        if stage is None:
            src, dst, index = kv_out, kv_back, kv_heads
        else:
            src, dst, index = q_out.at[stage], q_in.at[stage], stage
        return pltpu.make_async_remote_copy(
            src_ref=src.at[slot_rows(to), :],
            dst_ref=dst.at[slot_rows(dst_block), :],
            send_sem=row_ssem.at[index, s],
            recv_sem=row_rsem.at[index, s],
            device_id=(to, my_head),
            device_id_type=MESH,
        )

    def head_copies(stage, s, dst_head):
        to = lax.rem(my_head + s, heads)
        rows = pl.ds(pl.multiple_of(to * out_rows, out_rows), out_rows)
        if stage is None:
            triples = (
                (hkv.at[rows, :kv_cols], outk_ref.at[:, cols(dst_head, kv_cols)], kv_heads),
                (hkv.at[rows, kv_cols:], outv_ref.at[:, cols(dst_head, kv_cols)], kv_heads + 1),
            )
        else:
            triples = (
                (hq.at[stage, rows, :], outq_ref.at[:, cols(dst_head * kv_heads + stage, width)], stage),
            )
        return [
            pltpu.make_async_remote_copy(
                src_ref=src,
                dst_ref=dst,
                send_sem=head_ssem.at[index, s],
                recv_sem=head_rsem.at[index, s],
                device_id=(me, to),
                device_id_type=MESH,
            )
            for src, dst, index in triples
        ]

    def start_kv(n, _):
        for dist in range(1, DOC_BLOCKS + 1):
            for which in range(2):
                kv_copy(n, dist, which).start()
        return 0

    lax.fori_loop(0, kv_heads, start_kv, 0)

    q_pos = me * length + lax.broadcasted_iota(jnp.int32, (1, length), 1)
    begins = jnp.zeros((1, length), jnp.int32)
    first = jnp.int32(0)
    for i in range(lens_ref.shape[0]):
        begins = jnp.where(q_pos >= first, jnp.maximum(begins, first), begins)
        first = first + lens_ref[i]
    for dist in range(DOC_BLOCKS + 1):
        k_pos = (me - dist) * length + lax.broadcasted_iota(jnp.int32, (length, length), 0)
        seen = (k_pos <= q_pos) & (k_pos >= begins)
        bias[dist] = jnp.where(seen, 0.0, -jnp.inf).astype(f32)

    before = (
        lax.broadcasted_iota(jnp.int32, (length, length), 0)
        <= lax.broadcasted_iota(jnp.int32, (length, length), 1)
    ).astype(f32).astype(bf16)
    mine = lri_ref[pl.ds(me, 1), :]
    block_start = length * lax.broadcasted_iota(jnp.int32, (blocks, length), 0)
    owner = ((mine >= block_start) & (mine < block_start + length)).astype(f32)
    counts = jnp.dot(owner.astype(bf16), before, preferred_element_type=f32)
    block_base = (cap * lax.broadcasted_iota(jnp.int32, (blocks, length), 0)).astype(f32)
    slot = jnp.sum(owner * (block_base + counts - 1.0), axis=0, keepdims=True)
    slot_ids = lax.broadcasted_iota(jnp.int32, (slots, length), 0).astype(f32)
    send_pick[...] = (slot_ids == slot).astype(f32).astype(bf16)
    all_rows = lri_ref[...]
    base = me * length
    landing = ((all_rows >= base) & (all_rows < base + length)).astype(f32)
    landed = jnp.dot(landing.astype(bf16), before, preferred_element_type=f32)
    rank = jnp.where(landing > 0.5, landed - 1.0, -1.0)
    place_ids = lax.broadcasted_iota(jnp.int32, (length, length), 0)
    rank_ids = lax.broadcasted_iota(jnp.int32, (cap, length), 0).astype(f32)
    for i in range(blocks):
        at_place = (place_ids == all_rows[i : i + 1] - base).astype(f32).astype(bf16)
        at_rank = (rank_ids == rank[i : i + 1]).astype(f32).astype(bf16)
        land_t[i * cap : (i + 1) * cap, :] = lax.dot_general(
            at_rank, at_place, NT, preferred_element_type=f32
        )
    land_pick[...] = jnp.transpose(land_t[...]).astype(bf16)

    def start_rows(stage):
        def body(s, _):
            row_copy(stage, s, me).start()
            return 0

        lax.fori_loop(1, blocks, body, 0)

    def head_group(n, _):
        def stack(ref):
            return jnp.concatenate(
                [
                    ref[:, pl.ds(pl.multiple_of(n * width + g * d, d), d)]
                    for g in range(groups)
                ],
                axis=0,
            )

        qs, dos = stack(q_ref), stack(do_ref)
        product = dos.astype(f32) * stack(o_ref).astype(f32)
        delta = lax.dot_general(
            jnp.ones((8, d), f32),
            product,
            NT,
            precision=lax.Precision.HIGHEST,
            preferred_element_type=f32,
        )[0:1]
        lse2 = lse_ref[n] * LOG2E
        dq = None
        for dist in range(DOC_BLOCKS + 1):
            if dist == 0:
                kd, vd = k_ref[:, cols(n, d)], v_ref[:, cols(n, d)]
            else:
                for which in range(2):
                    kv_copy(n, dist, which).wait_recv()
                kd, vd = kv_in[n, dist - 1, 0], kv_in[n, dist - 1, 1]
            scores = lax.dot_general(kd, qs, NT, preferred_element_type=f32)
            mask = jnp.concatenate([bias[dist]] * groups, axis=1)
            weights = jnp.exp2(scores * (scale * LOG2E) - lse2 + mask)
            grad_w = lax.dot_general(vd, dos, NT, preferred_element_type=f32)
            grad_s = (weights * (grad_w - delta) * scale).astype(bf16)
            dv = jnp.dot(weights.astype(bf16), dos, preferred_element_type=f32)
            dk = jnp.dot(grad_s, qs, preferred_element_type=f32)
            term = lax.dot_general(grad_s, kd, TN, preferred_element_type=f32)
            dq = term if dq is None else dq + term
            if dist == 0:
                own_part[n, 0] = dk
                own_part[n, 1] = dv
            else:
                part_out[n, dist - 1, 0] = dk.astype(bf16)
                part_out[n, dist - 1, 1] = dv.astype(bf16)
                for which in range(2):
                    part_copy(n, dist, which).start()
        dq = dq.astype(bf16)
        for g in range(groups):
            q_out[n, :, g * d : (g + 1) * d] = jnp.dot(
                send_pick[...], dq[g * length : (g + 1) * length], preferred_element_type=f32
            ).astype(bf16)
        start_rows(n)
        return 0

    lax.fori_loop(0, kv_heads, head_group, 0)

    for n in range(kv_heads):
        for which in range(2):
            total = own_part[n, which]
            for dist in range(1, DOC_BLOCKS + 1):
                part_copy(n, dist, which).wait_recv()
                total = total + part_in[n, dist - 1, which].astype(f32)
            at = which * kv_cols + n * d
            kv_out[:, at : at + d] = jnp.dot(
                send_pick[...], total.astype(bf16), preferred_element_type=f32
            ).astype(bf16)
    start_rows(None)

    my_rows = pl.ds(pl.multiple_of(my_head * out_rows, out_rows), out_rows)

    def finish_rows(stage):
        def body(s, _):
            row_copy(stage, s, peer(-s)).wait_recv()
            return 0

        lax.fori_loop(1, blocks, body, 0)
        if stage is None:
            kv_back[slot_rows(me), :] = kv_out[slot_rows(me), :]
            hkv[...] = jnp.dot(
                land_pick[...], kv_back[...], preferred_element_type=f32
            ).astype(bf16)
        else:
            q_in[stage, slot_rows(me), :] = q_out[stage, slot_rows(me), :]
            hq[stage] = jnp.dot(
                land_pick[...], q_in[stage], preferred_element_type=f32
            ).astype(bf16)

        def send(s, _):
            for copy in head_copies(stage, s, my_head):
                copy.start()
            return 0

        lax.fori_loop(1, heads, send, 0)
        if stage is None:
            outk_ref[:, cols(my_head, kv_cols)] = hkv[my_rows, :kv_cols]
            outv_ref[:, cols(my_head, kv_cols)] = hkv[my_rows, kv_cols:]
        else:
            outq_ref[:, cols(my_head * kv_heads + stage, width)] = hq[stage, my_rows, :]

    def finish_q(n, _):
        finish_rows(n)
        return 0

    lax.fori_loop(0, kv_heads, finish_q, 0)
    finish_rows(None)

    def settle(stage):
        def arrive(s, _):
            for copy in head_copies(stage, s, lax.rem(my_head - s + heads, heads)):
                copy.wait_recv()
                copy.wait_send()
            return 0

        def sent(s, _):
            row_copy(stage, s, me).wait_send()
            return 0

        lax.fori_loop(1, heads, arrive, 0)
        lax.fori_loop(1, blocks, sent, 0)

    def settle_q(n, _):
        settle(n)
        for dist in range(1, DOC_BLOCKS + 1):
            for which in range(2):
                kv_copy(n, dist, which).wait_send()
                part_copy(n, dist, which).wait_send()
        return 0

    lax.fori_loop(0, kv_heads, settle_q, 0)
    settle(None)


def per_device(
    blocks,
    heads,
    query_head_rows,
    key_head_rows,
    value_head_rows,
    forward_output,
    cotangent,
    logsumexp,
    document_lengths,
    linear_row_index,
):
    length, q_cols = query_head_rows.shape
    kv_cols = key_head_rows.shape[1]
    d = HEAD_SIZE
    n = kv_cols // d
    width = q_cols // n
    cap = max(16, 2 * length // blocks)
    slots = blocks * cap
    rows = length // heads
    bf16, f32 = jnp.bfloat16, jnp.float32
    vmem = pl.BlockSpec(memory_space=pltpu.VMEM)
    dma = pltpu.SemaphoreType.DMA
    return pl.pallas_call(
        functools.partial(kernel, blocks, heads, cap),
        out_shape=(
            jax.ShapeDtypeStruct((rows, q_cols * heads), bf16),
            jax.ShapeDtypeStruct((rows, kv_cols * heads), bf16),
            jax.ShapeDtypeStruct((rows, kv_cols * heads), bf16),
        ),
        in_specs=[vmem] * 6 + [pl.BlockSpec(memory_space=pltpu.SMEM), vmem],
        out_specs=(vmem,) * 3,
        scratch_shapes=[
            pltpu.VMEM((n, DOC_BLOCKS, 2, length, d), bf16),
            pltpu.VMEM((DOC_BLOCKS + 1, length, length), f32),
            pltpu.VMEM((slots, length), bf16),
            pltpu.VMEM((slots, length), f32),
            pltpu.VMEM((length, slots), bf16),
            pltpu.VMEM((n, DOC_BLOCKS, 2, length, d), bf16),
            pltpu.VMEM((n, DOC_BLOCKS, 2, length, d), bf16),
            pltpu.VMEM((n, 2, length, d), f32),
            pltpu.VMEM((n, slots, width), bf16),
            pltpu.VMEM((n, slots, width), bf16),
            pltpu.VMEM((slots, 2 * kv_cols), bf16),
            pltpu.VMEM((slots, 2 * kv_cols), bf16),
            pltpu.VMEM((n, length, width), bf16),
            pltpu.VMEM((length, 2 * kv_cols), bf16),
            dma((n, DOC_BLOCKS, 2)),
            dma((n, DOC_BLOCKS, 2)),
            dma((n, DOC_BLOCKS, 2)),
            dma((n, DOC_BLOCKS, 2)),
            dma((n + 1, blocks)),
            dma((n + 1, blocks)),
            dma((n + 2, heads)),
            dma((n + 2, heads)),
        ],
        compiler_params=pltpu.CompilerParams(
            collective_id=0, has_side_effects=True, vmem_limit_bytes=56 * 2**20
        ),
    )(
        query_head_rows,
        key_head_rows,
        value_head_rows,
        forward_output,
        cotangent,
        logsumexp.reshape(n, 1, -1),
        document_lengths,
        linear_row_index.reshape(blocks, length),
    )


def solution(mesh):
    placed = (
        P("ctx", "head"),
        P("ctx", "head"),
        P("ctx", "head"),
        P("ctx", "head"),
        P("ctx", "head"),
        P("head", "ctx"),
        P(),
        P(),
    )
    rows = P(("ctx", "head"), None)
    return jax.shard_map(
        functools.partial(per_device, mesh.shape["ctx"], mesh.shape["head"]),
        mesh=mesh,
        in_specs=placed,
        out_specs=(rows, rows, rows),
        check_vma=False,
    )
```
